512 devices in a mesh: dp: 4 (over x), seq: 32 (over z, core), head: 4 (over y).
Axes of the slice: x: 4, y: 4, z: 16, core: 2. Of those that a mesh axis runs over, the one named last changes fastest.
Arguments:
- txt_qkv: bfloat16 [32, 256, 3, 2048], P('dp', 'seq', None, 'head'), may hold values from -6 to 6
- img_qkv: bfloat16 [32, 1792, 3, 2048], P('dp', 'seq', None, 'head'), may hold values from -6 to 6
- txt_grad_out: bfloat16 [32, 256, 2048], P('dp', 'seq', 'head'), may hold values from -6 to 6
- img_grad_out: bfloat16 [32, 1792, 2048], P('dp', 'seq', 'head'), may hold values from -6 to 6
- caption_len: int32 [32], P('dp'), may hold values from 1 to 256, as said below
- norm_gains: float32 [4, 128], replicated, may hold values from 0.5 to 6
Outputs:
- txt_out: bfloat16 [32, 256, 2048], P('dp', 'seq', 'head')
- img_out: bfloat16 [32, 1792, 2048], P('dp', 'seq', 'head')
- txt_grads: bfloat16 [32, 256, 3, 2048], P('dp', 'seq', None, 'head')
- img_grads: bfloat16 [32, 1792, 3, 2048], P('dp', 'seq', None, 'head')
- gain_grad: float32 [4, 128], replicated
The draws below stay inside these ranges and needn't reach their ends.
Inputs may be any that keep to these rules, and one draw needn't show every extreme that they name: `caption_len`: caption slots from a sample's length on are padding; in every draw some sample fills all 256 slots.
All inputs are finite; a program needn't handle non-finite values.
Results may differ from the reference program's by a relative error of at most 0.029.
The reference program's roundings to bfloat16 on the way count: a program that leaves them out, or rounds other values in their place, can miss the bound.
Values may be sent and summed in bfloat16 or wider, within the bound.
A program may use at most 64 MiB of HBM per device.

```python
import math
import jax
import jax.numpy as jnp
from jax import lax

DHEAD = 128
HEADS = 16
TXT = 256
IMG = 1792
BATCH = 32


def draw_img_qkv(key, part):
    key = jax.random.fold_in(key, 11)
    first_key = jax.random.fold_in(key, 0)
    full_shape = (BATCH, IMG, 3, HEADS * DHEAD)
    return jnp.clip(jax.random.normal(first_key, full_shape, jnp.float32), -6.0, 6.0).astype(jnp.bfloat16)


def draw_norm_gains(key, part):
    key = jax.random.fold_in(key, 12)
    return jnp.exp(jax.random.uniform(key, (4, DHEAD), jnp.float32, -0.6931, 0.6931))


def draw_caption_len(key, part):
    key = jax.random.fold_in(key, 13)
    first_key, second_key = jax.random.split(key)
    drawn = jax.random.randint(first_key, (BATCH,), 1, TXT + 1)
    chosen = jax.random.randint(second_key, (), 0, BATCH)
    return drawn.at[chosen].set(TXT).astype(jnp.int32)


def steps_of(key, extent, cuts, low, largest):
    def one(axis_at, shards_of):
        heights = jax.random.uniform(jax.random.fold_in(jax.random.fold_in(key, 6), axis_at), (shards_of,), jnp.float32, low / len(cuts), largest / len(cuts))
        return jnp.repeat(jnp.exp(heights), extent[axis_at] // shards_of).reshape((-1,) + (1,) * (len(extent) - axis_at - 1))

    factor_of = one(*cuts[0])
    for cut in cuts[1:]:
        factor_of = factor_of * one(*cut)
    return factor_of


def centred(rng, shape, scale, limit, shards=(), kind=jnp.bfloat16):
    array = jax.random.normal(rng, shape, jnp.float32) * scale
    if len(shards) > 0:
        array = steps_of(rng, shape, shards, -0.22, 0.18) * array
    return jnp.clip(array, min=-limit, max=limit).astype(kind)


def setup_inputs(seed: int = 0) -> dict:
    arg_keys = jax.random.split(jax.random.key(seed), 7)
    txt_qkv = centred(arg_keys[0], (BATCH, TXT, 3, HEADS * DHEAD), 1.0, 6.0, ((0, 4), (1, 32), (3, 4)))
    img_qkv = draw_img_qkv(jax.random.fold_in(arg_keys[6], 71), 0)
    txt_grad_out = centred(arg_keys[2], (BATCH, TXT, HEADS * DHEAD), 1.0, 6.0, ((0, 4), (1, 32), (2, 4)))
    img_grad_out = centred(arg_keys[3], (BATCH, IMG, HEADS * DHEAD), 1.0, 6.0, ((0, 4), (1, 32), (2, 4)))
    caption_len = draw_caption_len(jax.random.fold_in(arg_keys[6], 71), 0)
    norm_gains = draw_norm_gains(jax.random.fold_in(arg_keys[6], 71), 0)
    return {"txt_qkv": txt_qkv, "img_qkv": img_qkv, "txt_grad_out": txt_grad_out, "img_grad_out": img_grad_out, "caption_len": caption_len, "norm_gains": norm_gains}


EPSILON = 1e-06

def rms_forward(raw_part, text_rows, gain_text, gain_image):
    raw_values = raw_part.astype(jnp.float32).reshape(raw_part.shape[0], -1, DHEAD)
    inverse = lax.rsqrt(lax.optimization_barrier(jnp.mean(raw_values * raw_values, axis=-1)) + EPSILON)
    normed = raw_values * inverse[..., None]
    row_gain = jnp.where(text_rows[:, None], gain_text[None, :], gain_image[None, :])
    scaled = (normed * row_gain[:, None, :]).astype(jnp.bfloat16)
    return (normed, inverse, row_gain, scaled)

def rms_backward(grad_scaled, normed, inverse, row_gain, text_rows):
    grad_values = grad_scaled.astype(jnp.float32)
    grad_normed = grad_values * row_gain[:, None, :]
    inner = lax.optimization_barrier(jnp.mean(grad_normed * normed, axis=-1, keepdims=True))
    grad_raw = (inverse[..., None] * (grad_normed - normed * inner)).astype(jnp.bfloat16)
    per_row = lax.optimization_barrier(jnp.sum(grad_values * normed, axis=1))
    text_part = lax.optimization_barrier(jnp.sum(jnp.where(text_rows[:, None], per_row, 0.0), axis=0))
    image_part = lax.optimization_barrier(jnp.sum(jnp.where(text_rows[:, None], 0.0, per_row), axis=0))
    return (grad_raw, text_part, image_part)

def head_pass(query_head, key_head, value_head, cot_head, key_alive):
    score_scale = 1.0 / math.sqrt(DHEAD)
    scores = jnp.dot(query_head, key_head.T, preferred_element_type=jnp.float32) * score_scale
    masked = jnp.where(key_alive[None, :], scores, -jnp.inf)
    peak = lax.optimization_barrier(jnp.max(masked, axis=-1, keepdims=True))
    totals = lax.optimization_barrier(jnp.sum(jnp.exp(masked - peak), axis=-1, keepdims=True))
    log_total = peak + jnp.log(totals)
    weights = jnp.where(key_alive[None, :], jnp.exp(scores - log_total), 0.0)
    weights_low = weights.astype(jnp.bfloat16)
    attended = jnp.dot(weights_low, value_head, preferred_element_type=jnp.float32).astype(jnp.bfloat16)
    row_delta = lax.optimization_barrier(jnp.sum(cot_head.astype(jnp.float32) * attended.astype(jnp.float32), axis=-1, keepdims=True))
    grad_weights = jnp.dot(cot_head, value_head.T, preferred_element_type=jnp.float32)
    grad_scores = (weights * (grad_weights - row_delta)).astype(jnp.bfloat16)
    grad_query = (jnp.dot(grad_scores, key_head, preferred_element_type=jnp.float32) * score_scale).astype(jnp.bfloat16)
    grad_key = (jnp.dot(grad_scores.T, query_head, preferred_element_type=jnp.float32) * score_scale).astype(jnp.bfloat16)
    grad_value = jnp.dot(weights_low.T, cot_head, preferred_element_type=jnp.float32).astype(jnp.bfloat16)
    return (attended, grad_query, grad_key, grad_value)

def to_rows(per_head):
    return jnp.transpose(per_head, (1, 0, 2))

def sample_pass(sample, norm_gains):
    txt_part, img_part, txt_cot, img_cot, length = sample
    joint_rows = jnp.concatenate([txt_part, img_part], axis=0)
    cotangent = jnp.concatenate([txt_cot, img_cot], axis=0)
    seq_len = TXT + IMG
    positions = jnp.arange(seq_len, dtype=jnp.int32)
    text_rows = positions < TXT
    key_alive = jnp.where(text_rows, positions < length, True)
    q_normed, q_inverse, q_gain, query_norm = rms_forward(joint_rows[:, 0], text_rows, norm_gains[2], norm_gains[0])
    k_normed, k_inverse, k_gain, key_norm = rms_forward(joint_rows[:, 1], text_rows, norm_gains[3], norm_gains[1])
    values = joint_rows[:, 2].reshape(seq_len, HEADS, DHEAD)
    cot_heads = cotangent.reshape(seq_len, HEADS, DHEAD)

    def per_head(operands):
        return head_pass(operands[0], operands[1], operands[2], operands[3], key_alive)
    stacked = (to_rows(query_norm), to_rows(key_norm), to_rows(values), to_rows(cot_heads))
    attended, grad_query, grad_key, grad_value = lax.map(per_head, stacked)
    grad_q_raw, q_text, q_image = rms_backward(to_rows(grad_query), q_normed, q_inverse, q_gain, text_rows)
    grad_k_raw, k_text, k_image = rms_backward(to_rows(grad_key), k_normed, k_inverse, k_gain, text_rows)
    grads = jnp.stack([grad_q_raw.reshape(seq_len, -1), grad_k_raw.reshape(seq_len, -1), to_rows(grad_value).reshape(seq_len, -1)], axis=1)
    out_rows = to_rows(attended).reshape(seq_len, -1)
    gain_terms = jnp.stack([q_image, k_image, q_text, k_text])
    return (out_rows, grads, gain_terms)

def reference(txt_qkv, img_qkv, txt_grad_out, img_grad_out, caption_len, norm_gains):

    def per_sample(sample):
        return sample_pass(sample, norm_gains)
    out_rows, grads, gain_terms = lax.map(per_sample, (txt_qkv, img_qkv, txt_grad_out, img_grad_out, caption_len))
    return (out_rows[:, :TXT], out_rows[:, TXT:], grads[:, :TXT], grads[:, TXT:], lax.optimization_barrier(jnp.sum(gain_terms, axis=0)))
```

```python
import functools
import math

import jax
import jax.numpy as jnp
from jax import lax
from jax.experimental import pallas as pl
from jax.experimental.pallas import tpu as pltpu
from jax.sharding import PartitionSpec as P

EPSILON = 1e-06
MESH = pl.DeviceIdType.MESH
F32 = jnp.float32
BF16 = jnp.bfloat16
GROUP = 4


def partners(slot, me, count):
    chips = count // 2
    hop = lax.div(slot + 2, 4)
    side = lax.div(lax.rem(slot + 2, 4), 2)
    move = hop * (1 - 2 * side)
    chip, core = lax.div(me, 2), lax.rem(lax.rem(me, 2) + lax.rem(slot, 2), 2)
    to = lax.rem(chip + move + chips, chips) * 2 + core
    source = lax.rem(chip - move + chips, chips) * 2 + core
    return to, source


def nt(a, b):
    return lax.dot_general(a, b, (((1,), (1,)), ((), ())), preferred_element_type=F32)


def nn(a, b):
    return lax.dot_general(a, b, (((1,), (0,)), ((), ())), preferred_element_type=F32)


def attend(
    count,
    samples,
    text_block,
    block,
    dhead,
    others,
    txt_hbm,
    img_hbm,
    txt_cot_hbm,
    img_cot_hbm,
    length_ref,
    gains_ref,
    returned,
    gain_out,
    txt,
    img,
    txt_cot,
    img_cot,
    outgoing,
    arrived,
    results,
    keys,
    keys_turned,
    values_turned,
    bias,
    scores,
    key_total,
    value_total,
    gain_home,
    gain_ring,
    gain_mine,
    gain_plane,
    stage_sem,
    in_send,
    in_recv,
    back_send,
    back_recv,
    ring_send,
    ring_recv,
    plane_send,
    plane_recv,
):
    me = lax.axis_index("seq")
    dp = lax.axis_index("dp")
    head = lax.axis_index("head")
    groups = count // samples
    tile = GROUP * block
    tiles = count // GROUP
    scale = 1.0 / math.sqrt(dhead)
    planes = others[0] * others[1]
    here = dp * others[1] + head

    staged = [
        pltpu.make_async_copy(source, target, stage_sem.at[i])
        for i, (source, target) in enumerate(
            ((img_hbm, img), (txt_hbm, txt), (img_cot_hbm, img_cot), (txt_cot_hbm, txt_cot))
        )
    ]
    for copy in staged:
        copy.start()

    def plane_device(step):
        other = lax.rem(here + step, planes)
        return (lax.div(other, others[1]), me, lax.rem(other, others[1]))

    barrier = pltpu.get_barrier_semaphore()

    def greet(slot, carry):
        to, _ = partners(slot, me, count)
        pl.semaphore_signal(barrier, inc=1, device_id=(dp, to, head), device_id_type=MESH)
        return carry

    def greet_plane(step, carry):
        pl.semaphore_signal(barrier, inc=1, device_id=plane_device(step), device_id_type=MESH)
        return carry

    lax.fori_loop(1, count, greet, 0)
    lax.fori_loop(1, planes, greet_plane, 0)

    def joined(text_part, image_part):
        return jnp.concatenate([text_part.astype(F32), image_part.astype(F32)], axis=0).astype(BF16)

    def pack_pair(first, read_first, read_second):
        def pack(target, carry):
            sample = lax.div(target, groups)
            column = pl.multiple_of(lax.rem(target, groups) * dhead, dhead)
            outgoing[target, first] = read_first(sample, column)
            outgoing[target, first + 1] = read_second(sample, column)
            return carry

        lax.fori_loop(0, count, pack, 0)
        arrived[0, first] = outgoing[me, first]
        arrived[0, first + 1] = outgoing[me, first + 1]

    def raw(which):
        def read(sample, column):
            at = pl.ds(column, dhead)
            return joined(txt[sample, which, :, at], img[sample, which, :, at])

        return read

    def cotangent(sample, column):
        at = pl.ds(column, dhead)
        return joined(txt_cot[sample, :, at], img_cot[sample, :, at])

    def inward(slot, part):
        to, _ = partners(slot, me, count)
        return pltpu.make_async_remote_copy(
            src_ref=outgoing.at[to, pl.ds(2 * part, 2)],
            dst_ref=arrived.at[slot, pl.ds(2 * part, 2)],
            send_sem=in_send.at[part, slot],
            recv_sem=in_recv.at[part, slot],
            device_id=(dp, to, head),
            device_id_type=MESH,
        )

    def outward(slot, part):
        _, source = partners(slot, me, count)
        return pltpu.make_async_remote_copy(
            src_ref=results.at[slot, pl.ds(2 * part, 2)],
            dst_ref=returned.at[me, pl.ds(2 * part, 2)],
            send_sem=back_send.at[part, slot],
            recv_sem=back_recv.at[part, me],
            device_id=(dp, source, head),
            device_id_type=MESH,
        )

    def home(source, part):
        return pltpu.make_async_remote_copy(
            src_ref=results.at[0, pl.ds(2 * part, 2)],
            dst_ref=returned.at[source, pl.ds(2 * part, 2)],
            send_sem=back_send.at[part, 0],
            recv_sem=back_recv.at[part, source],
            device_id=(dp, source, head),
            device_id_type=MESH,
        )

    def each(low, high, body):
        def step(index, carry):
            body(index)
            return carry

        lax.fori_loop(low, high, step, 0)

    staged[0].wait()
    staged[1].wait()
    pack_pair(0, raw(1), raw(2))
    pl.semaphore_wait(barrier, count - 1 + planes - 1)
    each(1, count, lambda slot: inward(slot, 0).start())
    staged[2].wait()
    staged[3].wait()
    pack_pair(2, raw(0), cotangent)
    each(1, count, lambda slot: inward(slot, 1).start())

    place = lax.broadcasted_iota(jnp.int32, (block, dhead), 0)
    is_text = place < text_block

    def gain_rows(text_gain, image_gain):
        one = jnp.where(
            is_text,
            jnp.broadcast_to(gains_ref[pl.ds(text_gain, 1), :], (block, dhead)),
            jnp.broadcast_to(gains_ref[pl.ds(image_gain, 1), :], (block, dhead)),
        )
        return jnp.concatenate([one] * GROUP, axis=0)

    query_gain = gain_rows(2, 0)
    key_gain = gain_rows(3, 1)
    length = length_ref[lax.div(me, groups)]

    def mask(slot):
        _, source = partners(slot, me, count)
        row = lax.broadcasted_iota(jnp.int32, (block, 1), 0)
        dead = jnp.logical_and(row < text_block, row + source * text_block >= length)
        bias[pl.ds(pl.multiple_of(slot * block, block), block), :] = jnp.where(dead, -jnp.inf, 0.0)

    each(0, count, mask)
    key_total[...] = jnp.zeros_like(key_total)
    value_total[...] = jnp.zeros_like(value_total)

    def rows_of(index):
        return pl.ds(pl.multiple_of(index * tile, tile), tile)

    def block_of(ref, index, part):
        return ref[pl.ds(index * GROUP, GROUP), part].reshape(tile, dhead)

    def normed(raw_rows):
        inverse = lax.rsqrt(jnp.mean(raw_rows * raw_rows, axis=-1, keepdims=True) + EPSILON)
        return raw_rows * inverse, inverse

    def split_sums(terms):
        parts = terms.reshape(GROUP, block, dhead)
        text_sum = jnp.sum(parts[:, :text_block].reshape(-1, dhead), axis=0, keepdims=True)
        image_sum = jnp.sum(parts[:, text_block:].reshape(-1, dhead), axis=0, keepdims=True)
        return text_sum, image_sum

    def raw_gradient(scaled_grad, rows, inverse, gain):
        grad_rows = scaled_grad * gain
        inner = jnp.mean(grad_rows * rows, axis=-1, keepdims=True)
        return (inverse * (grad_rows - rows * inner)).astype(BF16)

    def prepare(index):
        each(
            jnp.maximum(index * GROUP, 1),
            (index + 1) * GROUP,
            lambda slot: inward(slot, 0).wait_recv(),
        )
        rows, _ = normed(block_of(arrived, index, 0).astype(F32))
        scaled = rows * key_gain
        keys[rows_of(index), :] = scaled.astype(BF16)
        keys_turned[:, rows_of(index)] = scaled.T.astype(BF16)
        values_turned[:, rows_of(index)] = block_of(arrived, index, 1).astype(F32).T.astype(BF16)

    each(0, tiles, prepare)

    def one_tile(index, carry):
        text_gain, image_gain = carry
        each(
            jnp.maximum(index * GROUP, 1),
            (index + 1) * GROUP,
            lambda slot: inward(slot, 1).wait_recv(),
        )
        rows, inverse = normed(block_of(arrived, index, 2).astype(F32))
        query = (rows * query_gain).astype(BF16)
        cot = block_of(arrived, index, 3)

        def score(part, peak):
            at = rows_of(part)
            here_scores = nt(keys[at, :], query) * scale + bias[at, :]
            scores[at, :] = here_scores
            return jnp.maximum(peak, jnp.max(here_scores, axis=0, keepdims=True))

        peak = lax.fori_loop(0, tiles, score, jnp.full((1, tile), -jnp.inf, F32))

        def exponent(part, total):
            at = rows_of(part)
            power = jnp.exp(scores[at, :] - peak)
            scores[at, :] = power
            return total + jnp.sum(power, axis=0, keepdims=True)

        total = lax.fori_loop(0, tiles, exponent, jnp.zeros((1, tile), F32))
        share = 1.0 / total

        def weigh(part, attended):
            at = rows_of(part)
            weights = scores[at, :] * share
            scores[at, :] = weights
            low = weights.astype(BF16)
            value_total[at, :] += nn(low, cot)
            return attended + nn(values_turned[:, at], low)

        attended = lax.fori_loop(0, tiles, weigh, jnp.zeros((dhead, tile), F32))
        attended = attended.astype(BF16).astype(F32)
        delta = jnp.sum(attended * cot.astype(F32).T, axis=0, keepdims=True)

        def differentiate(part, grad_query):
            at = rows_of(part)
            grad_weights = nt(block_of(arrived, part, 1), cot)
            grad_scores = (scores[at, :] * (grad_weights - delta)).astype(BF16)
            key_total[at, :] += nn(grad_scores, query)
            return grad_query + nn(keys_turned[:, at], grad_scores)

        grad_query = lax.fori_loop(0, tiles, differentiate, jnp.zeros((dhead, tile), F32))
        grad_query = (grad_query * scale).astype(BF16).astype(F32).T
        text_sum, image_sum = split_sums(grad_query * rows)
        slots = pl.ds(index * GROUP, GROUP)
        results[slots, 0] = raw_gradient(grad_query, rows, inverse, query_gain).reshape(
            GROUP, block, dhead
        )
        results[slots, 1] = attended.T.astype(BF16).reshape(GROUP, block, dhead)
        each(
            jnp.maximum(index * GROUP, 1),
            (index + 1) * GROUP,
            lambda slot: outward(slot, 0).start(),
        )
        return (text_gain + text_sum, image_gain + image_sum)

    nothing = jnp.zeros((1, dhead), F32)
    query_text, query_image = lax.fori_loop(0, tiles, one_tile, (nothing, nothing))

    def finish(index, carry):
        text_gain, image_gain = carry
        at = rows_of(index)
        rows, inverse = normed(block_of(arrived, index, 0).astype(F32))
        grad_key = (key_total[at, :] * scale).astype(BF16).astype(F32)
        text_sum, image_sum = split_sums(grad_key * rows)
        slots = pl.ds(index * GROUP, GROUP)
        results[slots, 2] = raw_gradient(grad_key, rows, inverse, key_gain).reshape(
            GROUP, block, dhead
        )
        results[slots, 3] = value_total[at, :].astype(BF16).reshape(GROUP, block, dhead)
        return (text_gain + text_sum, image_gain + image_sum)

    key_text, key_image = lax.fori_loop(0, tiles, finish, (nothing, nothing))

    gain_home[...] = jnp.concatenate([query_image, key_image, query_text, key_text], axis=0)

    def ring_copy(slot):
        to, _ = partners(slot, me, count)
        return pltpu.make_async_remote_copy(
            src_ref=gain_home,
            dst_ref=gain_ring.at[me],
            send_sem=ring_send.at[slot],
            recv_sem=ring_recv.at[me],
            device_id=(dp, to, head),
            device_id_type=MESH,
        )

    def ring_arrival(slot):
        _, source = partners(slot, me, count)
        return pltpu.make_async_remote_copy(
            src_ref=gain_home,
            dst_ref=gain_ring.at[source],
            send_sem=ring_send.at[slot],
            recv_sem=ring_recv.at[source],
            device_id=(dp, source, head),
            device_id_type=MESH,
        )

    def plane_copy(step):
        return pltpu.make_async_remote_copy(
            src_ref=gain_mine,
            dst_ref=gain_plane.at[here],
            send_sem=plane_send.at[step],
            recv_sem=plane_recv.at[here],
            device_id=plane_device(step),
            device_id_type=MESH,
        )

    def plane_arrival(step):
        other = lax.rem(here + step, planes)
        return pltpu.make_async_remote_copy(
            src_ref=gain_mine,
            dst_ref=gain_plane.at[other],
            send_sem=plane_send.at[step],
            recv_sem=plane_recv.at[other],
            device_id=plane_device(step),
            device_id_type=MESH,
        )

    each(1, count, lambda slot: ring_copy(slot).start())
    each(1, count, lambda slot: outward(slot, 1).start())
    returned[me] = results[0]
    gain_ring[me] = gain_home[...]
    each(1, count, lambda slot: ring_arrival(slot).wait_recv())
    gain_mine[...] = jnp.sum(gain_ring[...], axis=0)
    each(1, planes, lambda step: plane_copy(step).start())
    gain_plane[here] = gain_mine[...]
    each(1, planes, lambda step: plane_arrival(step).wait_recv())
    gain_out[...] = jnp.sum(gain_plane[...], axis=0)

    def drain(slot):
        inward(slot, 0).wait_send()
        inward(slot, 1).wait_send()
        ring_copy(slot).wait_send()
        outward(slot, 0).wait_send()
        outward(slot, 1).wait_send()

    each(1, count, drain)
    each(1, planes, lambda step: plane_copy(step).wait_send())

    def collect(slot):
        to, _ = partners(slot, me, count)
        home(to, 0).wait_recv()
        home(to, 1).wait_recv()

    each(1, count, collect)


def unpack(groups, text_block, dhead, returned, txt_out, img_out, txt_grads, img_grads):
    for group in range(groups):
        at = pl.ds(group * dhead, dhead)
        for sample in range(txt_out.shape[0]):
            for part in range(4):
                rows = returned[sample * groups + group, part].astype(F32)
                text_rows = rows[:text_block].astype(BF16)
                image_rows = rows[text_block:].astype(BF16)
                if part == 1:
                    txt_out[sample, :, at] = text_rows
                    img_out[sample, :, at] = image_rows
                else:
                    place = max(part - 1, 0)
                    txt_grads[sample, place, :, at] = text_rows
                    img_grads[sample, place, :, at] = image_rows


def shards(others, txt_qkv, img_qkv, txt_grad_out, img_grad_out, caption_len, norm_gains):
    count = lax.axis_size("seq")
    samples, text_block = txt_qkv.shape[:2]
    image_block, width = img_qkv.shape[1], img_qkv.shape[3]
    dhead = norm_gains.shape[1]
    block = text_block + image_block
    groups = count // samples
    rows = count * block
    tile = GROUP * block
    planes = others[0] * others[1]
    txt = txt_qkv.transpose(0, 2, 1, 3)
    img = img_qkv.transpose(0, 2, 1, 3)
    wire = (count, 4, block, dhead)
    in_vmem = pl.BlockSpec(memory_space=pltpu.VMEM)
    anywhere = pl.BlockSpec(memory_space=pl.ANY)
    dma = pltpu.SemaphoreType.DMA
    returned, gain_grad = pl.pallas_call(
        functools.partial(attend, count, samples, text_block, block, dhead, others),
        out_shape=(
            jax.ShapeDtypeStruct(wire, BF16),
            jax.ShapeDtypeStruct((4, dhead), F32),
        ),
        in_specs=[anywhere] * 4 + [pl.BlockSpec(memory_space=pltpu.SMEM), in_vmem],
        out_specs=(in_vmem, in_vmem),
        scratch_shapes=[
            pltpu.VMEM(txt.shape, BF16),
            pltpu.VMEM(img.shape, BF16),
            pltpu.VMEM(txt_grad_out.shape, BF16),
            pltpu.VMEM(img_grad_out.shape, BF16),
            pltpu.VMEM(wire, BF16),
            pltpu.VMEM(wire, BF16),
            pltpu.VMEM(wire, BF16),
            pltpu.VMEM((rows, dhead), BF16),
            pltpu.VMEM((dhead, rows), BF16),
            pltpu.VMEM((dhead, rows), BF16),
            pltpu.VMEM((rows, 1), F32),
            pltpu.VMEM((rows, tile), F32),
            pltpu.VMEM((rows, dhead), F32),
            pltpu.VMEM((rows, dhead), F32),
            pltpu.VMEM((4, dhead), F32),
            pltpu.VMEM((count, 4, dhead), F32),
            pltpu.VMEM((4, dhead), F32),
            pltpu.VMEM((planes, 4, dhead), F32),
            dma((4,)),
            dma((2, count)),
            dma((2, count)),
            dma((2, count)),
            dma((2, count)),
            dma((count,)),
            dma((count,)),
            dma((planes,)),
            dma((planes,)),
        ],
        compiler_params=pltpu.CompilerParams(
            collective_id=0, has_side_effects=True, vmem_limit_bytes=44 * 2**20
        ),
        name="attend",
    )(txt, img, txt_grad_out, img_grad_out, caption_len, norm_gains)
    part = 4
    txt_out, img_out, txt_grads, img_grads = pl.pallas_call(
        functools.partial(unpack, groups, text_block, dhead),
        grid=(samples // part,),
        out_shape=(
            jax.ShapeDtypeStruct((samples, text_block, width), BF16),
            jax.ShapeDtypeStruct((samples, image_block, width), BF16),
            jax.ShapeDtypeStruct((samples, 3, text_block, width), BF16),
            jax.ShapeDtypeStruct((samples, 3, image_block, width), BF16),
        ),
        in_specs=[pl.BlockSpec((part * groups, 4, block, dhead), lambda i: (i, 0, 0, 0))],
        out_specs=(
            pl.BlockSpec((part, text_block, width), lambda i: (i, 0, 0)),
            pl.BlockSpec((part, image_block, width), lambda i: (i, 0, 0)),
            pl.BlockSpec((part, 3, text_block, width), lambda i: (i, 0, 0, 0)),
            pl.BlockSpec((part, 3, image_block, width), lambda i: (i, 0, 0, 0)),
        ),
        compiler_params=pltpu.CompilerParams(vmem_limit_bytes=32 * 2**20),
        name="unpack",
    )(returned)
    return (
        txt_out,
        img_out,
        txt_grads.transpose(0, 2, 1, 3),
        img_grads.transpose(0, 2, 1, 3),
        gain_grad,
    )


def solution(mesh):
    others = (mesh.shape["dp"], mesh.shape["head"])
    placed = (
        P("dp", "seq", None, "head"),
        P("dp", "seq", None, "head"),
        P("dp", "seq", "head"),
        P("dp", "seq", "head"),
        P("dp"),
        P(),
    )
    return jax.shard_map(
        functools.partial(shards, others),
        mesh=mesh,
        in_specs=placed,
        out_specs=(
            P("dp", "seq", "head"),
            P("dp", "seq", "head"),
            P("dp", "seq", None, "head"),
            P("dp", "seq", None, "head"),
            P(),
        ),
        check_vma=False,
    )
```

```python
import functools
import math

import jax
import jax.numpy as jnp
from jax import lax
from jax.experimental import pallas as pl
from jax.experimental.pallas import tpu as pltpu
from jax.sharding import PartitionSpec as P

EPSILON = 1e-06
MESH = pl.DeviceIdType.MESH
F32 = jnp.float32
BF16 = jnp.bfloat16
CUT0, CUT1 = 16, 25
GROUP = 4


def partners(slot, me, count):
    chips = count // 2
    slot = jnp.where(slot == 0, 0, count - slot)
    hop = lax.div(slot + 2, 4)
    side = lax.div(lax.rem(slot + 2, 4), 2)
    move = hop * (1 - 2 * side)
    chip, core = lax.div(me, 2), lax.rem(lax.rem(me, 2) + lax.rem(slot, 2), 2)
    to = lax.rem(chip + move + chips, chips) * 2 + core
    source = lax.rem(chip - move + chips, chips) * 2 + core
    return to, source


def nt(a, b):
    return lax.dot_general(a, b, (((1,), (1,)), ((), ())), preferred_element_type=F32)


def nn(a, b):
    return lax.dot_general(a, b, (((1,), (0,)), ((), ())), preferred_element_type=F32)


def attend(
    count,
    samples,
    text_block,
    block,
    dhead,
    others,
    txt_hbm,
    img_hbm,
    txt_cot_hbm,
    img_cot_hbm,
    length_hbm,
    gains_hbm,
    returned,
    gain_out,
    txt,
    img,
    txt_cot,
    img_cot,
    length_ref,
    gains_ref,
    outgoing,
    arrived,
    results,
    keys,
    keys_turned,
    values_turned,
    bias,
    scores,
    key_total,
    value_total,
    gain_home,
    gain_ring,
    gain_mine,
    gain_pair,
    gain_plane,
    stage_sem,
    in_send,
    in_recv,
    back_send,
    back_recv,
    ring_send,
    ring_recv,
    plane_send,
    plane_recv,
):
    me = lax.axis_index("seq")
    dp = lax.axis_index("dp")
    head = lax.axis_index("head")
    groups = count // samples
    tile = GROUP * block
    tiles = count // GROUP
    scale = 1.0 / math.sqrt(dhead)
    planes = others[0] * others[1]
    here = dp * others[1] + head

    staged = [
        pltpu.make_async_copy(source, target, stage_sem.at[i])
        for i, (source, target) in enumerate(
            (
                (img_hbm, img),
                (txt_hbm, txt),
                (img_cot_hbm, img_cot),
                (txt_cot_hbm, txt_cot),
                (length_hbm, length_ref),
                (gains_hbm, gains_ref),
            )
        )
    ]
    for copy in staged:
        copy.start()

    def plane_device(step):
        other = lax.rem(here + step, planes)
        return (lax.div(other, others[1]), me, lax.rem(other, others[1]))

    barrier = pltpu.get_barrier_semaphore()

    def greet(slot, carry):
        to, _ = partners(slot, me, count)
        pl.semaphore_signal(barrier, inc=1, device_id=(dp, to, head), device_id_type=MESH)
        return carry

    def greet_plane(step, carry):
        pl.semaphore_signal(barrier, inc=1, device_id=plane_device(step), device_id_type=MESH)
        return carry

    lax.fori_loop(1, count, greet, 0)
    lax.fori_loop(1, planes, greet_plane, 0)

    def joined(text_part, image_part):
        return jnp.concatenate([text_part.astype(F32), image_part.astype(F32)], axis=0).astype(BF16)

    def pack(target, first, read_first, read_second):
        sample = lax.div(target, groups)
        column = pl.multiple_of(lax.rem(target, groups) * dhead, dhead)
        outgoing[target, first] = read_first(sample, column)
        outgoing[target, first + 1] = read_second(sample, column)

    def pack_own(first, read_first, read_second):
        pack(me, first, read_first, read_second)
        arrived[0, first] = outgoing[me, first]
        arrived[0, first + 1] = outgoing[me, first + 1]

    def raw(which):
        def read(sample, column):
            at = pl.ds(column, dhead)
            return joined(txt[sample, which, :, at], img[sample, which, :, at])

        return read

    def cotangent(sample, column):
        at = pl.ds(column, dhead)
        return joined(txt_cot[sample, :, at], img_cot[sample, :, at])

    def inward(slot, part):
        to, _ = partners(slot, me, count)
        return pltpu.make_async_remote_copy(
            src_ref=outgoing.at[to, pl.ds(2 * part, 2)],
            dst_ref=arrived.at[slot, pl.ds(2 * part, 2)],
            send_sem=in_send.at[part, slot],
            recv_sem=in_recv.at[part, slot],
            device_id=(dp, to, head),
            device_id_type=MESH,
        )

    def outward(slot, part):
        _, source = partners(slot, me, count)
        return pltpu.make_async_remote_copy(
            src_ref=results.at[slot, pl.ds(2 * part, 2)],
            dst_ref=returned.at[me, pl.ds(2 * part, 2)],
            send_sem=back_send.at[part, slot],
            recv_sem=back_recv.at[part, me],
            device_id=(dp, source, head),
            device_id_type=MESH,
        )

    def home(source, part):
        return pltpu.make_async_remote_copy(
            src_ref=results.at[0, pl.ds(2 * part, 2)],
            dst_ref=returned.at[source, pl.ds(2 * part, 2)],
            send_sem=back_send.at[part, 0],
            recv_sem=back_recv.at[part, source],
            device_id=(dp, source, head),
            device_id_type=MESH,
        )

    def each(low, high, body):
        def step(index, carry):
            body(index)
            return carry

        lax.fori_loop(low, high, step, 0)

    def send_keys(slot):
        to, _ = partners(slot, me, count)
        pack(to, 0, raw(1), raw(2))
        inward(slot, 0).start()

    def send_queries(slot):
        to, _ = partners(slot, me, count)
        pack(to, 2, raw(0), cotangent)
        inward(slot, 1).start()

    staged[0].wait()
    staged[1].wait()
    pack_own(0, raw(1), raw(2))
    pl.semaphore_wait(barrier, count - 1 + planes - 1)
    each(1, count, send_keys)
    staged[2].wait()
    staged[3].wait()
    each(1, count, send_queries)
    pack_own(2, raw(0), cotangent)

    staged[4].wait()
    staged[5].wait()
    place = lax.broadcasted_iota(jnp.int32, (block, dhead), 0)
    is_text = place < text_block

    def gain_rows(text_gain, image_gain):
        one = jnp.where(
            is_text,
            jnp.broadcast_to(gains_ref[pl.ds(text_gain, 1), :], (block, dhead)),
            jnp.broadcast_to(gains_ref[pl.ds(image_gain, 1), :], (block, dhead)),
        )
        return jnp.concatenate([one] * GROUP, axis=0)

    query_gain = gain_rows(2, 0)
    key_gain = gain_rows(3, 1)
    length = length_ref[lax.div(me, groups)]

    def mask(slot):
        _, source = partners(slot, me, count)
        row = lax.broadcasted_iota(jnp.int32, (block, 1), 0)
        dead = jnp.logical_and(row < text_block, row + source * text_block >= length)
        bias[pl.ds(pl.multiple_of(slot * block, block), block), :] = jnp.where(dead, -jnp.inf, 0.0)

    each(0, count, mask)
    key_total[...] = jnp.zeros_like(key_total)
    value_total[...] = jnp.zeros_like(value_total)

    def rows_of(index):
        return pl.ds(pl.multiple_of(index * tile, tile), tile)

    def block_of(ref, index, part):
        return ref[pl.ds(index * GROUP, GROUP), part].reshape(tile, dhead)

    def normed(raw_rows):
        inverse = lax.rsqrt(jnp.mean(raw_rows * raw_rows, axis=-1, keepdims=True) + EPSILON)
        return raw_rows * inverse, inverse

    def split_sums(terms):
        parts = terms.reshape(GROUP, block, dhead)
        text_sum = jnp.sum(parts[:, :text_block].reshape(-1, dhead), axis=0, keepdims=True)
        image_sum = jnp.sum(parts[:, text_block:].reshape(-1, dhead), axis=0, keepdims=True)
        return text_sum, image_sum

    def raw_gradient(scaled_grad, rows, inverse, gain):
        grad_rows = scaled_grad * gain
        inner = jnp.mean(grad_rows * rows, axis=-1, keepdims=True)
        return (inverse * (grad_rows - rows * inner)).astype(BF16)

    def prepare(index):
        each(
            jnp.maximum(index * GROUP, 1),
            (index + 1) * GROUP,
            lambda slot: inward(slot, 0).wait_recv(),
        )
        rows, _ = normed(block_of(arrived, index, 0).astype(F32))
        scaled = rows * key_gain
        keys[rows_of(index), :] = scaled.astype(BF16)
        keys_turned[:, rows_of(index)] = scaled.T.astype(BF16)
        values_turned[:, rows_of(index)] = block_of(arrived, index, 1).astype(F32).T.astype(BF16)

    each(0, tiles, prepare)

    def one_tile(index, carry):
        text_gain, image_gain = carry
        each(
            jnp.maximum(index * GROUP, 1),
            (index + 1) * GROUP,
            lambda slot: inward(slot, 1).wait_recv(),
        )
        rows, inverse = normed(block_of(arrived, index, 2).astype(F32))
        query = (rows * query_gain).astype(BF16)
        cot = block_of(arrived, index, 3)

        def score(part, peak):
            at = rows_of(part)
            here_scores = nt(keys[at, :], query) * scale + bias[at, :]
            scores[at, :] = here_scores
            return jnp.maximum(peak, jnp.max(here_scores, axis=0, keepdims=True))

        peak = lax.fori_loop(0, tiles, score, jnp.full((1, tile), -jnp.inf, F32))

        def exponent(part, total):
            at = rows_of(part)
            power = jnp.exp(scores[at, :] - peak)
            scores[at, :] = power
            return total + jnp.sum(power, axis=0, keepdims=True)

        total = lax.fori_loop(0, tiles, exponent, jnp.zeros((1, tile), F32))
        share = 1.0 / total

        def weigh(part, attended):
            at = rows_of(part)
            weights = scores[at, :] * share
            scores[at, :] = weights
            low = weights.astype(BF16)
            value_total[at, :] += nn(low, cot)
            return attended + nn(values_turned[:, at], low)

        attended = lax.fori_loop(0, tiles, weigh, jnp.zeros((dhead, tile), F32))
        attended = attended.astype(BF16).astype(F32)
        delta = jnp.sum(attended * cot.astype(F32).T, axis=0, keepdims=True)

        def differentiate(part, grad_query):
            at = rows_of(part)
            grad_weights = nt(block_of(arrived, part, 1), cot)
            grad_scores = (scores[at, :] * (grad_weights - delta)).astype(BF16)
            key_total[at, :] += nn(grad_scores, query)
            return grad_query + nn(keys_turned[:, at], grad_scores)

        grad_query = lax.fori_loop(0, tiles, differentiate, jnp.zeros((dhead, tile), F32))
        grad_query = (grad_query * scale).astype(BF16).astype(F32).T
        text_sum, image_sum = split_sums(grad_query * rows)
        slots = pl.ds(index * GROUP, GROUP)
        results[slots, 0] = raw_gradient(grad_query, rows, inverse, query_gain).reshape(
            GROUP, block, dhead
        )
        results[slots, 1] = attended.T.astype(BF16).reshape(GROUP, block, dhead)
        each(
            jnp.maximum(index * GROUP, 1),
            (index + 1) * GROUP,
            lambda slot: outward(slot, 0).start(),
        )
        return (text_gain + text_sum, image_gain + image_sum)

    nothing = jnp.zeros((1, dhead), F32)
    query_text, query_image = lax.fori_loop(0, tiles, one_tile, (nothing, nothing))

    def finish(index, carry):
        text_gain, image_gain = carry
        at = rows_of(index)
        rows, inverse = normed(block_of(arrived, index, 0).astype(F32))
        grad_key = (key_total[at, :] * scale).astype(BF16).astype(F32)
        text_sum, image_sum = split_sums(grad_key * rows)
        slots = pl.ds(index * GROUP, GROUP)
        results[slots, 2] = raw_gradient(grad_key, rows, inverse, key_gain).reshape(
            GROUP, block, dhead
        )
        results[slots, 3] = value_total[at, :].astype(BF16).reshape(GROUP, block, dhead)
        return (text_gain + text_sum, image_gain + image_sum)

    key_text, key_image = lax.fori_loop(0, tiles, finish, (nothing, nothing))

    gain_home[...] = jnp.concatenate([query_image, key_image, query_text, key_text], axis=0)

    chip, core = lax.div(me, 2), lax.rem(me, 2)
    speaks = here == chip

    def ring_copy(slot):
        to, _ = partners(slot, me, count)
        return pltpu.make_async_remote_copy(
            src_ref=gain_mine,
            dst_ref=gain_ring.at[core],
            send_sem=ring_send.at[slot],
            recv_sem=ring_recv.at[core],
            device_id=(dp, to, head),
            device_id_type=MESH,
        )

    def ring_arrival(which):
        return pltpu.make_async_remote_copy(
            src_ref=gain_mine,
            dst_ref=gain_ring.at[which],
            send_sem=ring_send.at[0],
            recv_sem=ring_recv.at[which],
            device_id=(dp, 2 * here + which, head),
            device_id_type=MESH,
        )

    def plane_copy(turn, step):
        return pltpu.make_async_remote_copy(
            src_ref=gain_home if turn == 0 else gain_pair,
            dst_ref=gain_plane.at[turn, here],
            send_sem=plane_send.at[turn, step],
            recv_sem=plane_recv.at[turn, here],
            device_id=plane_device(step),
            device_id_type=MESH,
        )

    def plane_arrival(turn, step):
        other = lax.rem(here + step, planes)
        return pltpu.make_async_remote_copy(
            src_ref=gain_home if turn == 0 else gain_pair,
            dst_ref=gain_plane.at[turn, other],
            send_sem=plane_send.at[turn, step],
            recv_sem=plane_recv.at[turn, other],
            device_id=plane_device(step),
            device_id_type=MESH,
        )

    def send_back(low, high):
        each(low, high, lambda index: outward(index, 1).start())

    each(1, planes, lambda step: plane_copy(0, step).start())
    gain_plane[0, here] = gain_home[...]
    mine = pltpu.make_async_copy(results.at[0], returned.at[me], stage_sem.at[0])
    mine.start()
    send_back(1, CUT0)
    each(1, planes, lambda step: plane_arrival(0, step).wait_recv())
    gain_mine[...] = jnp.sum(gain_plane[0], axis=0)

    @pl.when(speaks)
    def _():
        each(1, count, lambda slot: ring_copy(slot).start())
        gain_ring[core] = gain_mine[...]

    send_back(CUT0, CUT1)
    for which in range(2):

        @pl.when(2 * here + which != me)
        def _():
            ring_arrival(which).wait_recv()

    gain_pair[...] = gain_ring[0] + gain_ring[1]
    each(1, planes, lambda step: plane_copy(1, step).start())
    gain_plane[1, here] = gain_pair[...]
    send_back(CUT1, count)
    each(1, planes, lambda step: plane_arrival(1, step).wait_recv())
    gain_out[...] = jnp.sum(gain_plane[1], axis=0)

    def drain(slot):
        inward(slot, 0).wait_send()
        inward(slot, 1).wait_send()
        outward(slot, 0).wait_send()
        outward(slot, 1).wait_send()

    each(1, count, drain)
    each(1, planes, lambda step: plane_copy(0, step).wait_send())
    each(1, planes, lambda step: plane_copy(1, step).wait_send())

    @pl.when(speaks)
    def _():
        each(1, count, lambda slot: ring_copy(slot).wait_send())


    def collect(slot):
        to, _ = partners(slot, me, count)
        home(to, 0).wait_recv()
        home(to, 1).wait_recv()

    each(1, count, collect)
    mine.wait()


def unpack(groups, text_block, dhead, returned, gain_sum, txt_out, img_out, txt_grads, img_grads, gain_grad):
    gain_grad[...] = gain_sum[...]
    for group in range(groups):
        at = pl.ds(group * dhead, dhead)
        for sample in range(txt_out.shape[0]):
            for part in range(4):
                rows = returned[sample * groups + group, part].astype(F32)
                text_rows = rows[:text_block].astype(BF16)
                image_rows = rows[text_block:].astype(BF16)
                if part == 1:
                    txt_out[sample, :, at] = text_rows
                    img_out[sample, :, at] = image_rows
                else:
                    place = max(part - 1, 0)
                    txt_grads[sample, place, :, at] = text_rows
                    img_grads[sample, place, :, at] = image_rows


def shards(others, txt_qkv, img_qkv, txt_grad_out, img_grad_out, caption_len, norm_gains):
    count = lax.axis_size("seq")
    samples, text_block = txt_qkv.shape[:2]
    image_block, width = img_qkv.shape[1], img_qkv.shape[3]
    dhead = norm_gains.shape[1]
    block = text_block + image_block
    groups = count // samples
    rows = count * block
    tile = GROUP * block
    planes = others[0] * others[1]
    txt = txt_qkv.transpose(0, 2, 1, 3)
    img = img_qkv.transpose(0, 2, 1, 3)
    wire = (count, 4, block, dhead)
    in_vmem = pl.BlockSpec(memory_space=pltpu.VMEM)
    in_hbm = pl.BlockSpec(memory_space=pltpu.HBM)
    dma = pltpu.SemaphoreType.DMA
    returned, gain_sum = pl.pallas_call(
        functools.partial(attend, count, samples, text_block, block, dhead, others),
        out_shape=(
            jax.ShapeDtypeStruct(wire, BF16),
            jax.ShapeDtypeStruct((4, dhead), F32),
        ),
        in_specs=[in_hbm] * 6,
        out_specs=(in_hbm, in_vmem),
        scratch_shapes=[
            pltpu.VMEM(txt.shape, BF16),
            pltpu.VMEM(img.shape, BF16),
            pltpu.VMEM(txt_grad_out.shape, BF16),
            pltpu.VMEM(img_grad_out.shape, BF16),
            pltpu.SMEM((samples,), jnp.int32),
            pltpu.VMEM((4, dhead), F32),
            pltpu.VMEM(wire, BF16),
            pltpu.VMEM(wire, BF16),
            pltpu.VMEM(wire, BF16),
            pltpu.VMEM((rows, dhead), BF16),
            pltpu.VMEM((dhead, rows), BF16),
            pltpu.VMEM((dhead, rows), BF16),
            pltpu.VMEM((rows, 1), F32),
            pltpu.VMEM((rows, tile), F32),
            pltpu.VMEM((rows, dhead), F32),
            pltpu.VMEM((rows, dhead), F32),
            pltpu.VMEM((4, dhead), F32),
            pltpu.VMEM((2, 4, dhead), F32),
            pltpu.VMEM((4, dhead), F32),
            pltpu.VMEM((4, dhead), F32),
            pltpu.VMEM((2, planes, 4, dhead), F32),
            dma((6,)),
            dma((2, count)),
            dma((2, count)),
            dma((2, count)),
            dma((2, count)),
            dma((count,)),
            dma((2,)),
            dma((2, planes)),
            dma((2, planes)),
        ],
        compiler_params=pltpu.CompilerParams(
            collective_id=0, has_side_effects=True, vmem_limit_bytes=60 * 2**20
        ),
        name="attend",
    )(txt, img, txt_grad_out, img_grad_out, caption_len, norm_gains)
    part = 4
    txt_out, img_out, txt_grads, img_grads, gain_grad = pl.pallas_call(
        functools.partial(unpack, groups, text_block, dhead),
        grid=(samples // part,),
        out_shape=(
            jax.ShapeDtypeStruct((samples, text_block, width), BF16),
            jax.ShapeDtypeStruct((samples, image_block, width), BF16),
            jax.ShapeDtypeStruct((samples, 3, text_block, width), BF16),
            jax.ShapeDtypeStruct((samples, 3, image_block, width), BF16),
            jax.ShapeDtypeStruct((4, dhead), F32),
        ),
        in_specs=[
            pl.BlockSpec((part * groups, 4, block, dhead), lambda i: (i, 0, 0, 0)),
            pl.BlockSpec((4, dhead), lambda i: (0, 0)),
        ],
        out_specs=(
            pl.BlockSpec((part, text_block, width), lambda i: (i, 0, 0)),
            pl.BlockSpec((part, image_block, width), lambda i: (i, 0, 0)),
            pl.BlockSpec((part, 3, text_block, width), lambda i: (i, 0, 0, 0)),
            pl.BlockSpec((part, 3, image_block, width), lambda i: (i, 0, 0, 0)),
            pl.BlockSpec((4, dhead), lambda i: (0, 0)),
        ),
        compiler_params=pltpu.CompilerParams(vmem_limit_bytes=60 * 2**20),
        name="unpack",
    )(returned, gain_sum)
    return (
        txt_out,
        img_out,
        txt_grads.transpose(0, 2, 1, 3),
        img_grads.transpose(0, 2, 1, 3),
        gain_grad,
    )


def solution(mesh):
    others = (mesh.shape["dp"], mesh.shape["head"])
    placed = (
        P("dp", "seq", None, "head"),
        P("dp", "seq", None, "head"),
        P("dp", "seq", "head"),
        P("dp", "seq", "head"),
        P("dp"),
        P(),
    )
    return jax.shard_map(
        functools.partial(shards, others),
        mesh=mesh,
        in_specs=placed,
        out_specs=(
            P("dp", "seq", "head"),
            P("dp", "seq", "head"),
            P("dp", "seq", None, "head"),
            P("dp", "seq", None, "head"),
            P(),
        ),
        check_vma=False,
    )
```

```python
import functools
import math

import jax
import jax.numpy as jnp
from jax import lax
from jax.experimental import pallas as pl
from jax.experimental.pallas import tpu as pltpu
from jax.sharding import PartitionSpec as P

EPSILON = 1e-06
MESH = pl.DeviceIdType.MESH
F32 = jnp.float32
BF16 = jnp.bfloat16
CUT0, CUT1 = 16, 25
GROUP = 4


def partners(slot, me, count):
    chips = count // 2
    slot = jnp.where(slot == 0, 0, count - slot)
    hop = lax.div(slot + 2, 4)
    side = lax.div(lax.rem(slot + 2, 4), 2)
    move = hop * (1 - 2 * side)
    chip, core = lax.div(me, 2), lax.rem(lax.rem(me, 2) + lax.rem(slot, 2), 2)
    to = lax.rem(chip + move + chips, chips) * 2 + core
    source = lax.rem(chip - move + chips, chips) * 2 + core
    return to, source


def nt(a, b):
    return lax.dot_general(a, b, (((1,), (1,)), ((), ())), preferred_element_type=F32)


def nn(a, b):
    return lax.dot_general(a, b, (((1,), (0,)), ((), ())), preferred_element_type=F32)


def attend(
    count,
    samples,
    text_block,
    block,
    dhead,
    others,
    txt_hbm,
    img_hbm,
    txt_cot_hbm,
    img_cot_hbm,
    length_hbm,
    gains_hbm,
    returned,
    gain_out,
    txt,
    img,
    txt_cot,
    img_cot,
    length_ref,
    gains_ref,
    outgoing,
    arrived,
    results,
    keys,
    keys_turned,
    values_turned,
    bias,
    scores,
    key_total,
    value_total,
    gain_home,
    gain_ring,
    gain_mine,
    gain_pair,
    gain_plane,
    stage_sem,
    in_send,
    in_recv,
    back_send,
    back_recv,
    ring_send,
    ring_recv,
    plane_send,
    plane_recv,
):
    me = lax.axis_index("seq")
    dp = lax.axis_index("dp")
    head = lax.axis_index("head")
    groups = count // samples
    tile = GROUP * block
    tiles = count // GROUP
    scale = 1.0 / math.sqrt(dhead)
    planes = others[0] * others[1]
    here = dp * others[1] + head

    staged = [
        pltpu.make_async_copy(source, target, stage_sem.at[i])
        for i, (source, target) in enumerate(
            (
                (img_hbm, img),
                (txt_hbm, txt),
                (img_cot_hbm, img_cot),
                (txt_cot_hbm, txt_cot),
                (length_hbm, length_ref),
                (gains_hbm, gains_ref),
            )
        )
    ]
    for copy in staged:
        copy.start()

    def plane_device(step):
        other = lax.rem(here + step, planes)
        return (lax.div(other, others[1]), me, lax.rem(other, others[1]))

    barrier = pltpu.get_barrier_semaphore()

    def greet(slot, carry):
        to, _ = partners(slot, me, count)
        pl.semaphore_signal(barrier, inc=1, device_id=(dp, to, head), device_id_type=MESH)
        return carry

    def greet_plane(step, carry):
        pl.semaphore_signal(barrier, inc=1, device_id=plane_device(step), device_id_type=MESH)
        return carry

    lax.fori_loop(1, count, greet, 0)
    lax.fori_loop(1, planes, greet_plane, 0)

    def joined(text_part, image_part):
        return jnp.concatenate([text_part.astype(F32), image_part.astype(F32)], axis=0).astype(BF16)

    def pack(target, first, read_first, read_second):
        sample = lax.div(target, groups)
        column = pl.multiple_of(lax.rem(target, groups) * dhead, dhead)
        outgoing[target, first] = read_first(sample, column)
        outgoing[target, first + 1] = read_second(sample, column)

    def pack_own(first, read_first, read_second):
        pack(me, first, read_first, read_second)
        arrived[0, first] = outgoing[me, first]
        arrived[0, first + 1] = outgoing[me, first + 1]

    def raw(which):
        def read(sample, column):
            at = pl.ds(column, dhead)
            return joined(txt[sample, which, :, at], img[sample, which, :, at])

        return read

    def cotangent(sample, column):
        at = pl.ds(column, dhead)
        return joined(txt_cot[sample, :, at], img_cot[sample, :, at])

    def inward(slot, part):
        to, _ = partners(slot, me, count)
        return pltpu.make_async_remote_copy(
            src_ref=outgoing.at[to, pl.ds(2 * part, 2)],
            dst_ref=arrived.at[slot, pl.ds(2 * part, 2)],
            send_sem=in_send.at[part, slot],
            recv_sem=in_recv.at[part, slot],
            device_id=(dp, to, head),
            device_id_type=MESH,
        )

    def outward(slot, part):
        _, source = partners(slot, me, count)
        return pltpu.make_async_remote_copy(
            src_ref=results.at[slot, pl.ds(2 * part, 2)],
            dst_ref=returned.at[me, pl.ds(2 * part, 2)],
            send_sem=back_send.at[part, slot],
            recv_sem=back_recv.at[part, me],
            device_id=(dp, source, head),
            device_id_type=MESH,
        )

    def home(source, part):
        return pltpu.make_async_remote_copy(
            src_ref=results.at[0, pl.ds(2 * part, 2)],
            dst_ref=returned.at[source, pl.ds(2 * part, 2)],
            send_sem=back_send.at[part, 0],
            recv_sem=back_recv.at[part, source],
            device_id=(dp, source, head),
            device_id_type=MESH,
        )

    def each(low, high, body):
        def step(index, carry):
            body(index)
            return carry

        lax.fori_loop(low, high, step, 0)

    def send_keys(slot):
        to, _ = partners(slot, me, count)
        pack(to, 0, raw(1), raw(2))
        inward(slot, 0).start()

    def send_queries(slot):
        to, _ = partners(slot, me, count)
        pack(to, 2, raw(0), cotangent)
        inward(slot, 1).start()

    staged[0].wait()
    staged[1].wait()
    pack_own(0, raw(1), raw(2))
    pl.semaphore_wait(barrier, count - 1 + planes - 1)
    each(1, count, send_keys)
    staged[2].wait()
    staged[3].wait()
    each(1, count, send_queries)
    pack_own(2, raw(0), cotangent)

    staged[4].wait()
    staged[5].wait()
    place = lax.broadcasted_iota(jnp.int32, (block, dhead), 0)
    is_text = place < text_block

    def gain_rows(text_gain, image_gain):
        one = jnp.where(
            is_text,
            jnp.broadcast_to(gains_ref[pl.ds(text_gain, 1), :], (block, dhead)),
            jnp.broadcast_to(gains_ref[pl.ds(image_gain, 1), :], (block, dhead)),
        )
        return jnp.concatenate([one] * GROUP, axis=0)

    query_gain = gain_rows(2, 0)
    key_gain = gain_rows(3, 1)
    length = length_ref[lax.div(me, groups)]

    def mask(slot):
        _, source = partners(slot, me, count)
        row = lax.broadcasted_iota(jnp.int32, (block, 1), 0)
        dead = jnp.logical_and(row < text_block, row + source * text_block >= length)
        bias[pl.ds(pl.multiple_of(slot * block, block), block), :] = jnp.where(dead, -jnp.inf, 0.0)

    each(0, count, mask)
    key_total[...] = jnp.zeros_like(key_total)
    value_total[...] = jnp.zeros_like(value_total)

    def rows_of(index):
        return pl.ds(pl.multiple_of(index * tile, tile), tile)

    def block_of(ref, index, part):
        return ref[pl.ds(index * GROUP, GROUP), part].reshape(tile, dhead)

    def normed(raw_rows):
        inverse = lax.rsqrt(jnp.mean(raw_rows * raw_rows, axis=-1, keepdims=True) + EPSILON)
        return raw_rows * inverse, inverse

    def split_sums(terms):
        parts = terms.reshape(GROUP, block, dhead)
        text_sum = jnp.sum(parts[:, :text_block].reshape(-1, dhead), axis=0, keepdims=True)
        image_sum = jnp.sum(parts[:, text_block:].reshape(-1, dhead), axis=0, keepdims=True)
        return text_sum, image_sum

    def raw_gradient(scaled_grad, rows, inverse, gain):
        grad_rows = scaled_grad * gain
        inner = jnp.mean(grad_rows * rows, axis=-1, keepdims=True)
        return (inverse * (grad_rows - rows * inner)).astype(BF16)

    def prepare(index):
        each(
            jnp.maximum(index * GROUP, 1),
            (index + 1) * GROUP,
            lambda slot: inward(slot, 0).wait_recv(),
        )
        rows, _ = normed(block_of(arrived, index, 0).astype(F32))
        scaled = rows * key_gain
        keys[rows_of(index), :] = scaled.astype(BF16)
        keys_turned[:, rows_of(index)] = scaled.T.astype(BF16)
        values_turned[:, rows_of(index)] = block_of(arrived, index, 1).astype(F32).T.astype(BF16)

    each(0, tiles, prepare)

    def one_tile(index, carry):
        text_gain, image_gain = carry
        each(
            jnp.maximum(index * GROUP, 1),
            (index + 1) * GROUP,
            lambda slot: inward(slot, 1).wait_recv(),
        )
        rows, inverse = normed(block_of(arrived, index, 2).astype(F32))
        query = (rows * query_gain).astype(BF16)
        cot = block_of(arrived, index, 3)

        def score(part, peak):
            at = rows_of(part)
            here_scores = nt(keys[at, :], query) * scale + bias[at, :]
            scores[at, :] = here_scores
            return jnp.maximum(peak, jnp.max(here_scores, axis=0, keepdims=True))

        peak = lax.fori_loop(0, tiles, score, jnp.full((1, tile), -jnp.inf, F32))

        def exponent(part, total):
            at = rows_of(part)
            power = jnp.exp(scores[at, :] - peak)
            scores[at, :] = power
            return total + jnp.sum(power, axis=0, keepdims=True)

        total = lax.fori_loop(0, tiles, exponent, jnp.zeros((1, tile), F32))
        share = 1.0 / total

        def weigh(part, attended):
            at = rows_of(part)
            weights = scores[at, :] * share
            scores[at, :] = weights
            low = weights.astype(BF16)
            value_total[at, :] += nn(low, cot)
            return attended + nn(values_turned[:, at], low)

        attended = lax.fori_loop(0, tiles, weigh, jnp.zeros((dhead, tile), F32))
        attended = attended.astype(BF16).astype(F32)
        delta = jnp.sum(attended * cot.astype(F32).T, axis=0, keepdims=True)

        def differentiate(part, grad_query):
            at = rows_of(part)
            grad_weights = nt(block_of(arrived, part, 1), cot)
            grad_scores = (scores[at, :] * (grad_weights - delta)).astype(BF16)
            key_total[at, :] += nn(grad_scores, query)
            return grad_query + nn(keys_turned[:, at], grad_scores)

        grad_query = lax.fori_loop(0, tiles, differentiate, jnp.zeros((dhead, tile), F32))
        grad_query = (grad_query * scale).astype(BF16).astype(F32).T
        text_sum, image_sum = split_sums(grad_query * rows)
        slots = pl.ds(index * GROUP, GROUP)
        results[slots, 0] = raw_gradient(grad_query, rows, inverse, query_gain).reshape(
            GROUP, block, dhead
        )
        results[slots, 1] = attended.T.astype(BF16).reshape(GROUP, block, dhead)
        each(
            jnp.maximum(index * GROUP, 1),
            (index + 1) * GROUP,
            lambda slot: outward(slot, 0).start(),
        )
        return (text_gain + text_sum, image_gain + image_sum)

    nothing = jnp.zeros((1, dhead), F32)
    query_text, query_image = lax.fori_loop(0, tiles, one_tile, (nothing, nothing))

    def finish(index, carry):
        text_gain, image_gain = carry
        at = rows_of(index)
        rows, inverse = normed(block_of(arrived, index, 0).astype(F32))
        grad_key = (key_total[at, :] * scale).astype(BF16).astype(F32)
        text_sum, image_sum = split_sums(grad_key * rows)
        slots = pl.ds(index * GROUP, GROUP)
        results[slots, 2] = raw_gradient(grad_key, rows, inverse, key_gain).reshape(
            GROUP, block, dhead
        )
        results[slots, 3] = value_total[at, :].astype(BF16).reshape(GROUP, block, dhead)
        return (text_gain + text_sum, image_gain + image_sum)

    key_text, key_image = lax.fori_loop(0, tiles, finish, (nothing, nothing))

    gain_home[...] = jnp.concatenate([query_image, key_image, query_text, key_text], axis=0)

    chip, core = lax.div(me, 2), lax.rem(me, 2)
    speaks = here == chip

    def ring_copy(slot):
        to, _ = partners(slot, me, count)
        return pltpu.make_async_remote_copy(
            src_ref=gain_mine,
            dst_ref=gain_ring.at[core],
            send_sem=ring_send.at[slot],
            recv_sem=ring_recv.at[core],
            device_id=(dp, to, head),
            device_id_type=MESH,
        )

    def ring_arrival(which):
        return pltpu.make_async_remote_copy(
            src_ref=gain_mine,
            dst_ref=gain_ring.at[which],
            send_sem=ring_send.at[0],
            recv_sem=ring_recv.at[which],
            device_id=(dp, 2 * here + which, head),
            device_id_type=MESH,
        )

    def plane_copy(turn, step):
        return pltpu.make_async_remote_copy(
            src_ref=gain_home if turn == 0 else gain_pair,
            dst_ref=gain_plane.at[turn, here],
            send_sem=plane_send.at[turn, step],
            recv_sem=plane_recv.at[turn, here],
            device_id=plane_device(step),
            device_id_type=MESH,
        )

    def plane_arrival(turn, step):
        other = lax.rem(here + step, planes)
        return pltpu.make_async_remote_copy(
            src_ref=gain_home if turn == 0 else gain_pair,
            dst_ref=gain_plane.at[turn, other],
            send_sem=plane_send.at[turn, step],
            recv_sem=plane_recv.at[turn, other],
            device_id=plane_device(step),
            device_id_type=MESH,
        )

    def send_back(low, high):
        each(low, high, lambda index: outward(index, 1).start())

    each(1, planes, lambda step: plane_copy(0, step).start())
    gain_plane[0, here] = gain_home[...]
    mine = pltpu.make_async_copy(results.at[0], returned.at[me], stage_sem.at[0])
    mine.start()
    send_back(1, CUT0)
    each(1, planes, lambda step: plane_arrival(0, step).wait_recv())
    gain_mine[...] = jnp.sum(gain_plane[0], axis=0)

    @pl.when(speaks)
    def _():
        each(1, count, lambda slot: ring_copy(slot).start())
        gain_ring[core] = gain_mine[...]

    send_back(CUT0, CUT1)
    for which in range(2):

        @pl.when(2 * here + which != me)
        def _():
            ring_arrival(which).wait_recv()

    gain_pair[...] = gain_ring[0] + gain_ring[1]
    each(1, planes, lambda step: plane_copy(1, step).start())
    gain_plane[1, here] = gain_pair[...]
    send_back(CUT1, count)
    def settle(slot):
        to, _ = partners(slot, me, count)
        inward(slot, 0).wait_send()
        inward(slot, 1).wait_send()
        outward(slot, 0).wait_send()
        home(to, 0).wait_recv()

    each(1, count, settle)
    each(1, planes, lambda step: plane_copy(0, step).wait_send())

    @pl.when(speaks)
    def _():
        each(1, count, lambda slot: ring_copy(slot).wait_send())

    each(1, planes, lambda step: plane_arrival(1, step).wait_recv())
    gain_out[...] = jnp.sum(gain_plane[1], axis=0)
    each(1, planes, lambda step: plane_copy(1, step).wait_send())
    mine.wait()

    def settle_last(slot):
        to, _ = partners(slot, me, count)
        outward(slot, 1).wait_send()
        home(to, 1).wait_recv()

    each(1, count, settle_last)


def unpack(groups, text_block, dhead, returned, gain_sum, txt_out, img_out, txt_grads, img_grads, gain_grad):
    gain_grad[...] = gain_sum[...]
    for group in range(groups):
        at = pl.ds(group * dhead, dhead)
        for sample in range(txt_out.shape[0]):
            for part in range(4):
                rows = returned[sample * groups + group, part].astype(F32)
                text_rows = rows[:text_block].astype(BF16)
                image_rows = rows[text_block:].astype(BF16)
                if part == 1:
                    txt_out[sample, :, at] = text_rows
                    img_out[sample, :, at] = image_rows
                else:
                    place = max(part - 1, 0)
                    txt_grads[sample, place, :, at] = text_rows
                    img_grads[sample, place, :, at] = image_rows


def shards(others, txt_qkv, img_qkv, txt_grad_out, img_grad_out, caption_len, norm_gains):
    count = lax.axis_size("seq")
    samples, text_block = txt_qkv.shape[:2]
    image_block, width = img_qkv.shape[1], img_qkv.shape[3]
    dhead = norm_gains.shape[1]
    block = text_block + image_block
    groups = count // samples
    rows = count * block
    tile = GROUP * block
    planes = others[0] * others[1]
    txt = txt_qkv.transpose(0, 2, 1, 3)
    img = img_qkv.transpose(0, 2, 1, 3)
    wire = (count, 4, block, dhead)
    in_vmem = pl.BlockSpec(memory_space=pltpu.VMEM)
    in_hbm = pl.BlockSpec(memory_space=pltpu.HBM)
    dma = pltpu.SemaphoreType.DMA
    returned, gain_sum = pl.pallas_call(
        functools.partial(attend, count, samples, text_block, block, dhead, others),
        out_shape=(
            jax.ShapeDtypeStruct(wire, BF16),
            jax.ShapeDtypeStruct((4, dhead), F32),
        ),
        in_specs=[in_hbm] * 6,
        out_specs=(in_hbm, in_vmem),
        scratch_shapes=[
            pltpu.VMEM(txt.shape, BF16),
            pltpu.VMEM(img.shape, BF16),
            pltpu.VMEM(txt_grad_out.shape, BF16),
            pltpu.VMEM(img_grad_out.shape, BF16),
            pltpu.SMEM((samples,), jnp.int32),
            pltpu.VMEM((4, dhead), F32),
            pltpu.VMEM(wire, BF16),
            pltpu.VMEM(wire, BF16),
            pltpu.VMEM(wire, BF16),
            pltpu.VMEM((rows, dhead), BF16),
            pltpu.VMEM((dhead, rows), BF16),
            pltpu.VMEM((dhead, rows), BF16),
            pltpu.VMEM((rows, 1), F32),
            pltpu.VMEM((rows, tile), F32),
            pltpu.VMEM((rows, dhead), F32),
            pltpu.VMEM((rows, dhead), F32),
            pltpu.VMEM((4, dhead), F32),
            pltpu.VMEM((2, 4, dhead), F32),
            pltpu.VMEM((4, dhead), F32),
            pltpu.VMEM((4, dhead), F32),
            pltpu.VMEM((2, planes, 4, dhead), F32),
            dma((6,)),
            dma((2, count)),
            dma((2, count)),
            dma((2, count)),
            dma((2, count)),
            dma((count,)),
            dma((2,)),
            dma((2, planes)),
            dma((2, planes)),
        ],
        compiler_params=pltpu.CompilerParams(
            collective_id=0, has_side_effects=True, vmem_limit_bytes=60 * 2**20
        ),
        name="attend",
    )(txt, img, txt_grad_out, img_grad_out, caption_len, norm_gains)
    part = 4
    txt_out, img_out, txt_grads, img_grads, gain_grad = pl.pallas_call(
        functools.partial(unpack, groups, text_block, dhead),
        grid=(samples // part,),
        out_shape=(
            jax.ShapeDtypeStruct((samples, text_block, width), BF16),
            jax.ShapeDtypeStruct((samples, image_block, width), BF16),
            jax.ShapeDtypeStruct((samples, 3, text_block, width), BF16),
            jax.ShapeDtypeStruct((samples, 3, image_block, width), BF16),
            jax.ShapeDtypeStruct((4, dhead), F32),
        ),
        in_specs=[
            pl.BlockSpec((part * groups, 4, block, dhead), lambda i: (i, 0, 0, 0)),
            pl.BlockSpec((4, dhead), lambda i: (0, 0)),
        ],
        out_specs=(
            pl.BlockSpec((part, text_block, width), lambda i: (i, 0, 0)),
            pl.BlockSpec((part, image_block, width), lambda i: (i, 0, 0)),
            pl.BlockSpec((part, 3, text_block, width), lambda i: (i, 0, 0, 0)),
            pl.BlockSpec((part, 3, image_block, width), lambda i: (i, 0, 0, 0)),
            pl.BlockSpec((4, dhead), lambda i: (0, 0)),
        ),
        compiler_params=pltpu.CompilerParams(vmem_limit_bytes=60 * 2**20),
        name="unpack",
    )(returned, gain_sum)
    return (
        txt_out,
        img_out,
        txt_grads.transpose(0, 2, 1, 3),
        img_grads.transpose(0, 2, 1, 3),
        gain_grad,
    )


def solution(mesh):
    others = (mesh.shape["dp"], mesh.shape["head"])
    placed = (
        P("dp", "seq", None, "head"),
        P("dp", "seq", None, "head"),
        P("dp", "seq", "head"),
        P("dp", "seq", "head"),
        P("dp"),
        P(),
    )
    return jax.shard_map(
        functools.partial(shards, others),
        mesh=mesh,
        in_specs=placed,
        out_specs=(
            P("dp", "seq", "head"),
            P("dp", "seq", "head"),
            P("dp", "seq", None, "head"),
            P("dp", "seq", None, "head"),
            P(),
        ),
        check_vma=False,
    )
```
